32 devices in a mesh: dom: 8 (over y, x, core), mode: 4 (over z).
Axes of the slice: x: 2, y: 2, z: 4, core: 2. Of those that a mesh axis runs over, the one named last changes fastest.
Arguments:
- source: float32 [32768], P('dom'), may hold values from -36 to 36
- mass: float32 [32768], P('dom'), may hold values from 0.3 to 3
- lambdas: float32 [16], P('mode'), may hold values from 0.05 to 4
- trace_basis: float32 [16, 16], replicated, may hold values from -3 to 3
- blocks: float32 [9, 64, 32768], P(None, None, 'dom'), may hold values from -0.01 to 2, as said below
- columns: int32 [512, 9], P('dom'), may hold values from 0 to 191, as said below
Outputs:
- trace_levels: float32 [16, 32768], P('mode', 'dom')
The draws below stay inside these ranges and needn't reach their ends.
Inputs may be any that keep to these rules, and one draw needn't show every extreme that they name: `columns`: slot 0 of cluster c names c itself; slots 1 to 4 name clusters of the same partition, or c itself where the block is zero; slot 5 + h names 64 + h * 32 + c when c < 32 and cluster c is coupled to cluster c of partition p + (-2, -1, 1, 2)[h], else c itself with a zero block. The number of coupled partitions differs between partitions. The pattern is symmetric. The operator assembled from blocks and columns is symmetric and strictly diagonally dominant with a positive diagonal.
All inputs are finite; a program needn't handle non-finite values.
Results may differ from the reference program's by a relative error of at most 0.00015.
Values sent between devices are 32-bit elements; how exact they have to be, the bound alone decides.
A program may use at most 128 MiB of HBM per device.

```python
import math
import jax
import jax.numpy as jnp
from jax import lax

CLUSTER = 64
CL = 64
IFC = 32
NB = 9
MODES = 16
LEVELS = 16
ITERS = 2
VERTS = 32768
N_DOM = 8


def pattern(key):
    perm_keys = jax.random.split(jax.random.fold_in(key, 11), N_DOM)

    def shuffle(subkey):
        return jax.random.permutation(subkey, CL)
    orders = jax.vmap(shuffle)(perm_keys).astype(jnp.int32)
    places = jnp.argsort(orders, axis=1).astype(jnp.int32)
    linked = (jax.random.randint(jax.random.fold_in(key, 12), (N_DOM, 2), 0, 4) > 0).astype(jnp.int32)
    linked = linked.at[0].set(1)
    partition = jnp.arange(N_DOM, dtype=jnp.int32)[:, None]
    owned = jnp.arange(CL, dtype=jnp.int32)[None, :]
    zeros_int = jnp.zeros((N_DOM, CL), jnp.int32)
    entries = [owned + zeros_int]
    present = [zeros_int + 1]
    peers = [partition + zeros_int]
    for offset in (-1, 1, -2, 2):
        target = places + offset
        inside = (target >= 0) & (target < CL)
        other = jnp.take_along_axis(orders, jnp.clip(target, 0, CL - 1), axis=1)
        entries.append(jnp.where(inside, other, owned + zeros_int))
        present.append(inside.astype(jnp.int32))
        peers.append(partition + zeros_int)
    for slot, offset in enumerate((-2, -1, 1, 2)):
        if offset > 0:
            flags = linked[:, offset - 1]
        else:
            flags = jnp.roll(linked[:, -offset - 1], -offset)
        inside = (owned < IFC) & (flags[:, None] > 0)
        entries.append(jnp.where(inside, CL + slot * IFC + owned, owned + zeros_int))
        present.append(inside.astype(jnp.int32))
        peers.append((partition + offset) % N_DOM + zeros_int)
    return (jnp.stack(entries, -1), jnp.stack(present, -1), jnp.stack(peers, -1))


def draw_columns(key, part):
    entries, present, peers = pattern(key)
    return entries.reshape(N_DOM * CL, NB).astype(jnp.int32)


def draw_blocks(key, part):
    entries, present, peers = pattern(key)
    key = jax.random.fold_in(key, 21)
    owned = jnp.arange(CL, dtype=jnp.int32)[None, :, None]
    partition = jnp.arange(N_DOM, dtype=jnp.int32)[:, None, None]
    global_row = partition * CL + owned + jnp.zeros((N_DOM, CL, NB), jnp.int32)
    partner = jnp.where(entries >= CL, owned, entries)
    global_col = peers * CL + partner
    lower = jnp.minimum(global_row, global_col)
    upper = jnp.maximum(global_row, global_col)
    reach = 1.4 / (9 * CLUSTER - 1)

    def one_tile(first, second):
        subkey = jax.random.fold_in(jax.random.fold_in(key, first), second)
        return jax.random.uniform(subkey, (CLUSTER, CLUSTER), jnp.float32, -reach, 0.0)
    uniform_tiles = jax.vmap(one_tile)(lower.reshape(-1), upper.reshape(-1))
    uniform_tiles = uniform_tiles.reshape(N_DOM, CL, NB, CLUSTER, CLUSTER)
    swapped = jnp.swapaxes(uniform_tiles, -1, -2)
    tiles = jnp.where((global_row > global_col)[..., None, None], swapped, uniform_tiles)
    identity = jnp.eye(CLUSTER, dtype=jnp.float32)
    diagonal_values = 1.5 + 0.5 * jax.random.uniform(jax.random.fold_in(key, 7), (N_DOM, CL, 1, 1, CLUSTER), jnp.float32)
    symmetric = 0.5 * (uniform_tiles + swapped)
    diagonal_tiles = symmetric * (1.0 - identity) + identity * diagonal_values
    slot_index = jnp.arange(NB, dtype=jnp.int32)[None, None, :, None, None]
    tiles = jnp.where(slot_index == 0, diagonal_tiles, tiles)
    tiles = tiles * present[..., None, None].astype(jnp.float32)
    return jnp.transpose(tiles, (2, 4, 0, 1, 3)).reshape(NB, CLUSTER, N_DOM * CL * CLUSTER)


def draw_source(key, part):
    key = jax.random.fold_in(key, 31)
    position = jnp.arange(VERTS, dtype=jnp.float32) / (VERTS - 1)
    smooth = 4.0 + 2.0 * jnp.sin(18.849556 * position)
    rough = 1.5 * jax.random.truncated_normal(key, -4.0, 4.0, (VERTS,), jnp.float32)
    values = (smooth + rough) * jnp.power(3.0, position)
    return values


def steps_of(key, extent, shards, low, largest):
    level = 1.0
    for dim, blocks in shards:
        draws = jax.random.uniform(jax.random.fold_in(jax.random.fold_in(key, 6), dim), (blocks,), jnp.float32, low / len(shards), largest / len(shards))
        level = level * jnp.repeat(jnp.exp(draws), extent[dim] // blocks).reshape((-1,) + (1,) * (len(extent) - 1 - dim))
    return level


def bell_draw(own_key, dims, width, bound, held_as=jnp.bfloat16):
    values = width * jax.random.normal(own_key, dims, jnp.float32)
    return jnp.clip(values, min=-bound, max=bound).astype(held_as)


def setup_inputs(seed: int = 0) -> dict:
    key_list = jax.random.split(jax.random.key(seed), 7)
    source = draw_source(jax.random.fold_in(key_list[6], 71), 0)
    mass = jnp.clip(jnp.exp(math.log(3.0) - 2.3025851 * jax.random.uniform(key_list[1], (VERTS,), jnp.float32) ** steps_of(key_list[1], (VERTS,), ((0, 8),), -0.2, 0.2)), 0.3, 3.0)
    lambdas = jnp.clip(jnp.exp(math.log(4.0) - 4.3820266 * jax.random.uniform(key_list[2], (MODES,), jnp.float32) ** steps_of(key_list[2], (MODES,), ((0, 4),), -0.2, 0.2)), 0.05, 4.0)
    trace_basis = bell_draw(key_list[3], (LEVELS, MODES), 0.5, 3.0, jnp.float32)
    blocks = draw_blocks(jax.random.fold_in(key_list[6], 71), 0)
    columns = draw_columns(jax.random.fold_in(key_list[6], 71), 0)
    return {"source": source, "mass": mass, "lambdas": lambdas, "trace_basis": trace_basis, "blocks": blocks, "columns": columns}


OFFSETS = (-2, -1, 1, 2)


def neighbour_table(columns):
    entries = columns.reshape(N_DOM, CL, NB)
    partition = jnp.arange(N_DOM, dtype=jnp.int32)[:, None, None]
    beyond = entries - CL
    slot_index = jnp.clip(beyond // IFC, 0, 3)
    offset_table = jnp.array(OFFSETS, dtype=jnp.int32)
    remote = ((partition + offset_table[slot_index]) % N_DOM) * CL + beyond % IFC
    result = jnp.where(entries >= CL, remote, partition * CL + entries)
    return result.reshape(N_DOM * CL, NB).astype(jnp.int32)


def apply_operator(field, blocks, table, shift_field):
    modes_all = field.shape[0]
    cluster_rows = field.reshape(modes_all, N_DOM * CL, CLUSTER)
    picked = cluster_rows[:, table, :]
    weights = blocks.reshape(NB, CLUSTER, N_DOM * CL, CLUSTER)
    product = jnp.einsum("sjci,mcsj->mci", weights, picked, precision=lax.Precision.HIGHEST)
    return product.reshape(modes_all, -1) + shift_field * field


def reference(source, mass, lambdas, trace_basis, blocks, columns):
    table = neighbour_table(columns)
    shift_field = lambdas[:, None] * mass[None, :]
    right_side = trace_basis[0][:, None] * (mass * source)[None, :]
    solution = jnp.zeros_like(right_side)
    residual = right_side
    direction = right_side
    norm_now = jnp.sum(residual * residual, axis=1)
    for number in range(ITERS):
        image = apply_operator(direction, blocks, table, shift_field)
        step_size = norm_now / jnp.sum(direction * image, axis=1)
        solution = solution + step_size[:, None] * direction
        if number + 1 < ITERS:
            residual = residual - step_size[:, None] * image
            norm_next = jnp.sum(residual * residual, axis=1)
            direction = residual + (norm_next / norm_now)[:, None] * direction
            norm_now = norm_next
    return jnp.dot(trace_basis, solution, precision=lax.Precision.HIGHEST)
```

```python
import functools

import jax
import jax.numpy as jnp
from jax import lax
from jax.experimental import pallas as pl
from jax.experimental.pallas import tpu as pltpu
from jax.sharding import PartitionSpec as P

LEVELS = 16
OFFSETS = (-2, -1, 1, 2)
OWN = 5
HIGHEST = lax.Precision.HIGHEST
MESH = pl.DeviceIdType.MESH
F32 = jnp.float32
BF16 = jnp.bfloat16


def halves(value):
    high = value.astype(BF16)
    return high, (value - high.astype(F32)).astype(BF16)


def dot(a, b, dims=((1,), (0,)), precision=None):
    return lax.dot_general(a, b, (dims, ((), ())), precision=precision, preferred_element_type=F32)


def fold(value):
    half = value.shape[0] // 2
    return jnp.concatenate([value[:half], value[half:]], axis=1)


def unfold(value):
    half = value.shape[1] // 2
    return jnp.concatenate([value[:, :half], value[:, half:]], axis=0)


def column_of(row):
    n = row.shape[1]
    eye = lax.broadcasted_iota(jnp.int32, (n, n), 0) == lax.broadcasted_iota(jnp.int32, (n, n), 1)
    spread = jnp.where(eye, jnp.broadcast_to(row, (n, n)), 0.0)
    return jnp.broadcast_to(jnp.sum(spread, axis=1, keepdims=True), (n, 128))


def kernel(
    n_dom, n_mode,
    source_ref, mass_ref, lam_ref, basis_ref, blocks_ref, cols_ref, out_ref,
    own_f32, far_f32, own_hi, own_lo, far_hi, far_lo, v_ref, acc_own, acc_far,
    lam_buf, far1_out, far1_in, far2_out, far2_in, sum1_out, sum1_in, sum2_out, sum2_in,
    load_sem, lam_send, lam_recv, far1_send, far1_recv, far2_send, far2_recv,
    sum1_send, sum1_recv, sum2_send, sum2_recv,
):
    me = lax.axis_index("dom")
    my_mode = lax.axis_index("mode")
    width = own_f32.shape[1]
    clusters = cols_ref.shape[0]
    shared = clusters // 2
    md = lam_ref.shape[1]
    levels = out_ref.shape[1]
    span = 1024
    far_chunks = shared * width // span
    own_chunks = clusters * width // span
    per_chunk = span // width

    loads = []
    for n in range(far_chunks):
        lanes = pl.ds(n * span, span)
        loads.append(pltpu.make_async_copy(
            blocks_ref.at[pl.ds(OWN, 4), :, lanes], far_f32.at[:, :, lanes], load_sem.at[n]))
    for n in range(own_chunks):
        lanes = pl.ds(n * span, span)
        loads.append(pltpu.make_async_copy(
            blocks_ref.at[pl.ds(0, OWN), :, lanes], own_f32.at[:, :, lanes], load_sem.at[far_chunks + n]))
    for load in loads:
        load.start()

    barrier = pltpu.get_barrier_semaphore()
    for d in range(1, n_dom):
        pl.semaphore_signal(barrier, inc=1, device_id=(lax.rem(me + d, n_dom), my_mode), device_id_type=MESH)
    for d in range(1, n_mode):
        pl.semaphore_signal(barrier, inc=1, device_id=(me, lax.rem(my_mode + d, n_mode)), device_id_type=MESH)

    f_nat = mass_ref[...] * source_ref[...]
    m_nat = mass_ref[...]
    w_nat = m_nat * f_nat
    pairs = clusters // 2
    pair_row = lax.broadcasted_iota(jnp.int32, (pairs, clusters), 0)
    cluster_col = lax.broadcasted_iota(jnp.int32, (pairs, clusters), 1)
    even = (cluster_col == 2 * pair_row).astype(F32)
    odd = (cluster_col == 2 * pair_row + 1).astype(F32)

    def across(nat):
        first = dot(nat, even, ((0,), (0,)), HIGHEST)
        second = dot(nat, odd, ((0,), (0,)), HIGHEST)
        return first[:width] + second[width:]

    def back(vec):
        first = dot(even, vec, ((1,), (1,)), HIGHEST)
        second = dot(odd, vec, ((1,), (1,)), HIGHEST)
        return jnp.concatenate([first, second], axis=1)

    m_t = across(m_nat)
    f_t = across(f_nat)
    w_t = m_t * f_t

    def spread(vectors):
        high = [v.astype(BF16).astype(F32) for v in vectors]
        packed = jnp.concatenate(high + [v - h for v, h in zip(vectors, high)], axis=1)
        lane = lax.rem(lax.broadcasted_iota(jnp.int32, packed.shape, 1), clusters)
        n = packed.shape[1]

        def place(g, carry):
            v_ref[pl.ds(pl.multiple_of(g * width, width), width), 0:n] = jnp.where(lane == g, packed, 0.0).astype(BF16)
            return carry
        lax.fori_loop(0, clusters, place, 0, unroll=8)

    spread([f_t, w_t])

    lam_row = lam_ref[...]
    lam_tile = jnp.concatenate([column_of(lam_row), jnp.zeros((8 - md, 128), F32)], axis=0)
    lam_buf[0] = lam_tile
    wait_for = n_dom - 1 + n_mode - 1
    pl.semaphore_wait(barrier, wait_for)

    sends = []
    lam_copies = []
    for d in range(1, n_mode):
        copy = pltpu.make_async_remote_copy(
            src_ref=lam_buf.at[0], dst_ref=lam_buf.at[d], send_sem=lam_send.at[d], recv_sem=lam_recv.at[d],
            device_id=(me, lax.rem(my_mode + d, n_mode)), device_id_type=MESH)
        copy.start()
        lam_copies.append(copy)

    def far_copies(out_buf, in_buf, send, recv):
        copies = []
        for h, offset in enumerate(OFFSETS):
            copies.append(pltpu.make_async_remote_copy(
                src_ref=out_buf.at[h], dst_ref=in_buf.at[h], send_sem=send.at[h], recv_sem=recv.at[h],
                device_id=(lax.rem(me + n_dom + offset, n_dom), my_mode), device_id_type=MESH))
        return copies

    def sum_copies(out_buf, in_buf, send, recv):
        copies = []
        for d in range(1, n_dom):
            copies.append(pltpu.make_async_remote_copy(
                src_ref=out_buf, dst_ref=in_buf.at[d - 1], send_sem=send.at[d - 1], recv_sem=recv.at[d - 1],
                device_id=(lax.rem(me + d, n_dom), my_mode), device_id_type=MESH))
        return copies

    def product(count, chunks, first_load, full, high, low, acc, n, first_pass):
        for c in range(chunks):
            lanes = pl.ds(c * span, span)
            if first_pass:
                loads[first_load + c].wait()
                hi, lo = halves(full[:, :, lanes].reshape(count * width, span))
                high[:, lanes] = hi
                low[:, lanes] = lo
            else:
                hi, lo = high[:, lanes], low[:, lanes]
            right = v_ref[lanes, 0:n]
            part = dot(hi, right) + dot(lo, right)
            if c:
                acc[:, 0:n] += part
            else:
                acc[:, 0:n] = part
        return acc[:, 0:n // 2] + acc[:, n // 2:n]

    cluster_lane = lax.broadcasted_iota(jnp.int32, (clusters, clusters), 1)

    def collect(terms, vectors):
        total = terms[:width]
        high, low = halves(terms[width:])
        moved = None
        for s in range(1, OWN):
            hot = (cols_ref[:, s:s + 1] == cluster_lane).astype(F32).astype(BF16)
            if vectors == 2:
                zero = jnp.zeros_like(hot)
                hot = jnp.concatenate([jnp.concatenate([hot, zero], 1), jnp.concatenate([zero, hot], 1)], 0)
            rows = slice((s - 1) * width, s * width)
            part = dot(high[rows], hot) + dot(low[rows], hot)
            moved = part if moved is None else moved + part
        return total + moved

    def widen(value):
        return jnp.concatenate([value, jnp.zeros((width, clusters - shared), F32)], axis=1)

    n1 = 4 * clusters
    terms = product(4, far_chunks, 0, far_f32, far_hi, far_lo, acc_far, n1, True)
    far1 = far_copies(far1_out, far1_in, far1_send, far1_recv)
    for h in range(4):
        rows = terms[h * width:(h + 1) * width]
        both = jnp.concatenate([rows[:, :shared], rows[:, clusters:clusters + shared]], axis=1)
        far1_out[h] = fold(both)
        far1[h].start()
    terms = product(OWN, own_chunks, far_chunks, own_f32, own_hi, own_lo, acc_own, n1, True)
    image = collect(terms, 2)
    for h in range(4):
        far1[h].wait_recv()
    arrived = unfold(far1_in[0] + far1_in[1] + far1_in[2] + far1_in[3])
    u_t = image[:, :clusters] + widen(arrived[:, :shared])
    q_t = image[:, clusters:] + widen(arrived[:, shared:])

    f_v, w_v, m_v, u_v, q_v = fold(f_t), fold(w_t), fold(m_t), fold(u_t), fold(q_t)

    def over(value):
        return jnp.sum(value, axis=0, keepdims=True)

    sum1_out[...] = jnp.concatenate(
        [over(f_v * f_v), over(f_v * u_v), over(f_v * w_v), jnp.zeros((5, 128), F32)], axis=0)
    sum1 = sum_copies(sum1_out, sum1_in, sum1_send, sum1_recv)
    for copy in sum1:
        copy.start()

    n2 = 2 * clusters
    spread([u_t])
    terms = product(4, far_chunks, 0, far_f32, far_hi, far_lo, acc_far, n2, False)
    far2 = far_copies(far2_out, far2_in, far2_send, far2_recv)
    for h in range(4):
        far2_out[h] = fold(fold(terms[h * width:(h + 1) * width, :shared]))
        far2[h].start()
    terms = product(OWN, own_chunks, far_chunks, own_f32, own_hi, own_lo, acc_own, n2, False)
    image = collect(terms, 1)

    for copy in lam_copies:
        copy.wait_recv()
    lam = jnp.zeros((md * n_mode, 128), F32)
    part_row = lax.broadcasted_iota(jnp.int32, (md * n_mode, 128), 0) // md
    for d in range(n_mode):
        own = lax.rem(my_mode + n_mode - d, n_mode)
        tiled = jnp.concatenate([lam_buf[d][:md]] * n_mode, axis=0)
        lam = jnp.where(part_row == own, tiled, lam)
    t = column_of(basis_ref[0:1, :])
    t2 = t * t

    for copy in sum1:
        copy.wait_recv()
    sums = sum1_out[...]
    for d in range(n_dom - 1):
        sums = sums + sum1_in[d]
    sums = jnp.broadcast_to(jnp.sum(sums, axis=1, keepdims=True), (8, 128))
    rr0 = t2 * sums[0:1]
    alpha = rr0 / (t2 * (sums[1:2] + lam * sums[2:3]))
    alpha_lam = alpha * lam

    for h in range(4):
        far2[h].wait_recv()
    arrived = unfold(unfold(far2_in[0] + far2_in[1] + far2_in[2] + far2_in[3]))
    p_v = fold(image + widen(arrived))

    squares, curves = [], []
    for k in range(md * n_mode):
        a, al = alpha[k:k + 1], alpha_lam[k:k + 1]
        r = f_v - a * u_v - al * w_v
        image_r = u_v - a * p_v - al * q_v + lam[k:k + 1] * (m_v * r)
        squares.append(over(r * r))
        curves.append(over(r * image_r))
    sum2_out[...] = jnp.concatenate(squares + curves, axis=0)
    sum2 = sum_copies(sum2_out, sum2_in, sum2_send, sum2_recv)
    for copy in sum2:
        copy.start()

    u_nat = back(u_t)
    rows = [column_of(basis_ref[pl.ds(my_mode * levels + level, 1), :]) for level in range(levels)]

    for copy in sum2:
        copy.wait_recv()
    sums = sum2_out[...]
    for d in range(n_dom - 1):
        sums = sums + sum2_in[d]
    modes = md * n_mode
    sums = jnp.broadcast_to(jnp.sum(sums, axis=1, keepdims=True), (2 * modes, 128))
    rr1 = t2 * sums[:modes]
    beta = rr1 / rr0
    alpha1 = rr1 / (t2 * sums[modes:] - beta * (rr1 / alpha))
    coef_f = t * (alpha + alpha1 * (1.0 + beta))
    coef_u = -t * (alpha1 * alpha)
    coef_w = coef_u * lam
    for level in range(levels):
        c_f, c_u, c_w = (over(rows[level] * c) for c in (coef_f, coef_u, coef_w))
        out_ref[:, level, :] = c_f * f_nat + c_u * u_nat + c_w * w_nat

    for copy in lam_copies + far1 + far2 + sum1 + sum2:
        copy.wait_send()


def solution(mesh):
    n_dom, n_mode = mesh.shape["dom"], mesh.shape["mode"]

    def body(source, mass, lambdas, trace_basis, blocks, columns):
        slots, width, vertices = blocks.shape
        clusters = columns.shape[0]
        shared = clusters // 2
        md = lambdas.shape[0]
        levels = LEVELS // n_mode
        lines = vertices // 128
        vmem = pl.BlockSpec(memory_space=pltpu.VMEM)
        dma = pltpu.SemaphoreType.DMA
        chunks = vertices // 1024 + shared * width // 1024
        result = pl.pallas_call(
            functools.partial(kernel, n_dom, n_mode),
            out_shape=jax.ShapeDtypeStruct((lines, levels, 128), F32),
            in_specs=[vmem, vmem, vmem, vmem, pl.BlockSpec(memory_space=pl.ANY), vmem],
            out_specs=vmem,
            scratch_shapes=[
                pltpu.VMEM((OWN, width, vertices), F32),
                pltpu.VMEM((slots - OWN, width, shared * width), F32),
                pltpu.VMEM((OWN * width, vertices), BF16),
                pltpu.VMEM((OWN * width, vertices), BF16),
                pltpu.VMEM(((slots - OWN) * width, shared * width), BF16),
                pltpu.VMEM(((slots - OWN) * width, shared * width), BF16),
                pltpu.VMEM((vertices, 4 * clusters), BF16),
                pltpu.VMEM((OWN * width, 4 * clusters), F32),
                pltpu.VMEM(((slots - OWN) * width, 4 * clusters), F32),
                pltpu.VMEM((n_mode, 8, 128), F32),
                pltpu.VMEM((4, width // 2, 2 * clusters), F32),
                pltpu.VMEM((4, width // 2, 2 * clusters), F32),
                pltpu.VMEM((4, width // 4, 4 * shared), F32),
                pltpu.VMEM((4, width // 4, 4 * shared), F32),
                pltpu.VMEM((8, 128), F32),
                pltpu.VMEM((n_dom - 1, 8, 128), F32),
                pltpu.VMEM((2 * md * n_mode, 128), F32),
                pltpu.VMEM((n_dom - 1, 2 * md * n_mode, 128), F32),
                dma((chunks,)),
                dma((n_mode,)), dma((n_mode,)),
                dma((4,)), dma((4,)), dma((4,)), dma((4,)),
                dma((n_dom - 1,)), dma((n_dom - 1,)), dma((n_dom - 1,)), dma((n_dom - 1,)),
            ],
            compiler_params=pltpu.CompilerParams(
                collective_id=0, has_side_effects=True, vmem_limit_bytes=48 * 1024 * 1024),
        )(
            source.reshape(lines, 128), mass.reshape(lines, 128), lambdas.reshape(1, md),
            trace_basis, blocks, columns,
        )
        return jnp.transpose(result, (1, 0, 2)).reshape(levels, vertices)

    in_specs = (P("dom"), P("dom"), P("mode"), P(), P(None, None, "dom"), P("dom", None))
    return jax.shard_map(body, mesh=mesh, in_specs=in_specs, out_specs=P("mode", "dom"), check_vma=False)
```

```python
import functools

import jax
import jax.numpy as jnp
from jax import lax
from jax.experimental import pallas as pl
from jax.experimental.pallas import tpu as pltpu
from jax.sharding import PartitionSpec as P

LEVELS = 16
OFFSETS = (-2, -1, 1, 2)
OWN = 5
HIGHEST = lax.Precision.HIGHEST
MESH = pl.DeviceIdType.MESH
F32 = jnp.float32
BF16 = jnp.bfloat16


def halves(value):
    high = value.astype(BF16)
    return high, (value - high.astype(F32)).astype(BF16)


def dot(a, b, dims=((1,), (0,)), precision=None):
    return lax.dot_general(a, b, (dims, ((), ())), precision=precision, preferred_element_type=F32)


def fold(value):
    half = value.shape[0] // 2
    return jnp.concatenate([value[:half], value[half:]], axis=1)


def unfold(value):
    half = value.shape[1] // 2
    return jnp.concatenate([value[:, :half], value[:, half:]], axis=0)


def column_of(row):
    n = row.shape[1]
    eye = lax.broadcasted_iota(jnp.int32, (n, n), 0) == lax.broadcasted_iota(jnp.int32, (n, n), 1)
    spread = jnp.where(eye, jnp.broadcast_to(row, (n, n)), 0.0)
    return jnp.broadcast_to(jnp.sum(spread, axis=1, keepdims=True), (n, 128))


def kernel(
    n_dom, n_mode,
    source_hbm, mass_hbm, lam_hbm, basis_hbm, blocks_ref, cols_hbm, out_ref,
    source_ref, mass_ref, lam_ref, basis_ref, cols_ref,
    own_f32, far_f32, own_hi, own_lo, far_hi, far_lo, v_ref, acc_own, acc_far,
    lam_buf, far1_out, far1_in, far2_out, far2_in, sum1_out, sum1_in, sum2_out, sum2_in,
    small_sem, load_sem, lam_send, lam_recv, far1_send, far1_recv, far2_send, far2_recv,
    sum1_send, sum1_recv, sum2_send, sum2_recv,
):
    me = lax.axis_index("dom")
    my_mode = lax.axis_index("mode")
    width = own_f32.shape[1]
    clusters = cols_ref.shape[1]
    shared = clusters // 2
    md = lam_ref.shape[1]
    levels = out_ref.shape[1]
    span = 1024
    far_chunks = shared * width // span
    own_chunks = clusters * width // span
    per_chunk = span // width

    small = [
        pltpu.make_async_copy(src, dst, small_sem.at[n])
        for n, (src, dst) in enumerate((
            (source_hbm, source_ref), (mass_hbm, mass_ref), (lam_hbm, lam_ref),
            (basis_hbm, basis_ref), (cols_hbm, cols_ref)))
    ]
    for copy in small:
        copy.start()
    loads = []
    for n in range(far_chunks):
        lanes = pl.ds(n * span, span)
        loads.append(pltpu.make_async_copy(
            blocks_ref.at[pl.ds(OWN, 4), :, lanes], far_f32.at[:, :, lanes], load_sem.at[n]))
    for n in range(own_chunks):
        lanes = pl.ds(n * span, span)
        loads.append(pltpu.make_async_copy(
            blocks_ref.at[pl.ds(0, OWN), :, lanes], own_f32.at[:, :, lanes], load_sem.at[far_chunks + n]))
    for load in loads:
        load.start()

    barrier = pltpu.get_barrier_semaphore()
    for d in range(1, n_dom):
        pl.semaphore_signal(barrier, inc=1, device_id=(lax.rem(me + d, n_dom), my_mode), device_id_type=MESH)
    for d in range(1, n_mode):
        pl.semaphore_signal(barrier, inc=1, device_id=(me, lax.rem(my_mode + d, n_mode)), device_id_type=MESH)

    for copy in small:
        copy.wait()
    f_nat = mass_ref[...] * source_ref[...]
    m_nat = mass_ref[...]
    w_nat = m_nat * f_nat
    pairs = clusters // 2
    pair_row = lax.broadcasted_iota(jnp.int32, (pairs, clusters), 0)
    cluster_col = lax.broadcasted_iota(jnp.int32, (pairs, clusters), 1)
    even = (cluster_col == 2 * pair_row).astype(F32)
    odd = (cluster_col == 2 * pair_row + 1).astype(F32)

    def across(nat):
        first = dot(nat, even, ((0,), (0,)), HIGHEST)
        second = dot(nat, odd, ((0,), (0,)), HIGHEST)
        return first[:width] + second[width:]

    def back(vec):
        first = dot(even, vec, ((1,), (1,)), HIGHEST)
        second = dot(odd, vec, ((1,), (1,)), HIGHEST)
        return jnp.concatenate([first, second], axis=1)

    m_t = across(m_nat)
    f_t = across(f_nat)
    w_t = m_t * f_t

    def spread(vectors):
        high = [v.astype(BF16).astype(F32) for v in vectors]
        packed = jnp.concatenate(high + [v - h for v, h in zip(vectors, high)], axis=1)
        lane = lax.rem(lax.broadcasted_iota(jnp.int32, packed.shape, 1), clusters)
        n = packed.shape[1]

        def place(g, carry):
            v_ref[pl.ds(pl.multiple_of(g * width, width), width), 0:n] = jnp.where(lane == g, packed, 0.0).astype(BF16)
            return carry
        lax.fori_loop(0, clusters, place, 0, unroll=8)

    spread([f_t, w_t])

    lam_row = lam_ref[...]
    lam_tile = jnp.concatenate([column_of(lam_row), jnp.zeros((8 - md, 128), F32)], axis=0)
    lam_buf[0] = lam_tile
    wait_for = n_dom - 1 + n_mode - 1
    pl.semaphore_wait(barrier, wait_for)

    sends = []
    lam_copies = []
    for d in range(1, n_mode):
        copy = pltpu.make_async_remote_copy(
            src_ref=lam_buf.at[0], dst_ref=lam_buf.at[d], send_sem=lam_send.at[d], recv_sem=lam_recv.at[d],
            device_id=(me, lax.rem(my_mode + d, n_mode)), device_id_type=MESH)
        copy.start()
        lam_copies.append(copy)

    def far_copies(out_buf, in_buf, send, recv):
        copies = []
        for h, offset in enumerate(OFFSETS):
            copies.append(pltpu.make_async_remote_copy(
                src_ref=out_buf.at[h], dst_ref=in_buf.at[h], send_sem=send.at[h], recv_sem=recv.at[h],
                device_id=(lax.rem(me + n_dom + offset, n_dom), my_mode), device_id_type=MESH))
        return copies

    def sum_copies(out_buf, in_buf, send, recv):
        copies = []
        for d in range(1, n_dom):
            copies.append(pltpu.make_async_remote_copy(
                src_ref=out_buf, dst_ref=in_buf.at[d - 1], send_sem=send.at[d - 1], recv_sem=recv.at[d - 1],
                device_id=(lax.rem(me + d, n_dom), my_mode), device_id_type=MESH))
        return copies

    def product(count, chunks, first_load, full, high, low, acc, n, first_pass):
        for c in range(chunks):
            lanes = pl.ds(c * span, span)
            if first_pass:
                loads[first_load + c].wait()
                hi, lo = halves(full[:, :, lanes].reshape(count * width, span))
                high[:, lanes] = hi
                low[:, lanes] = lo
            else:
                hi, lo = high[:, lanes], low[:, lanes]
            right = v_ref[lanes, 0:n]
            part = dot(hi, right) + dot(lo, right)
            if c:
                acc[:, 0:n] += part
            else:
                acc[:, 0:n] = part
        return acc[:, 0:n // 2] + acc[:, n // 2:n]

    cluster_row = lax.broadcasted_iota(jnp.int32, (clusters, clusters), 0)

    def collect(terms, vectors):
        total = terms[:width]
        high, low = halves(terms[width:])
        moved = None
        for s in range(1, OWN):
            hot = (cols_ref[s:s + 1, :] == cluster_row).astype(F32).astype(BF16)
            if vectors == 2:
                zero = jnp.zeros_like(hot)
                hot = jnp.concatenate([jnp.concatenate([hot, zero], 1), jnp.concatenate([zero, hot], 1)], 0)
            rows = slice((s - 1) * width, s * width)
            part = dot(high[rows], hot, ((1,), (1,))) + dot(low[rows], hot, ((1,), (1,)))
            moved = part if moved is None else moved + part
        return total + moved

    def widen(value):
        return jnp.concatenate([value, jnp.zeros((width, clusters - shared), F32)], axis=1)

    n1 = 4 * clusters
    terms = product(4, far_chunks, 0, far_f32, far_hi, far_lo, acc_far, n1, True)
    far1 = far_copies(far1_out, far1_in, far1_send, far1_recv)
    for h in range(4):
        rows = terms[h * width:(h + 1) * width]
        both = jnp.concatenate([rows[:, :shared], rows[:, clusters:clusters + shared]], axis=1)
        far1_out[h] = fold(both)
        far1[h].start()
    terms = product(OWN, own_chunks, far_chunks, own_f32, own_hi, own_lo, acc_own, n1, True)
    image = collect(terms, 2)
    for h in range(4):
        far1[h].wait_recv()
    arrived = unfold(far1_in[0] + far1_in[1] + far1_in[2] + far1_in[3])
    u_t = image[:, :clusters] + widen(arrived[:, :shared])
    q_t = image[:, clusters:] + widen(arrived[:, shared:])

    f_v, w_v, m_v, u_v, q_v = fold(f_t), fold(w_t), fold(m_t), fold(u_t), fold(q_t)

    def over(value):
        return jnp.sum(value, axis=0, keepdims=True)

    sum1_out[...] = jnp.concatenate(
        [over(f_v * f_v), over(f_v * u_v), over(f_v * w_v), jnp.zeros((5, 128), F32)], axis=0)
    sum1 = sum_copies(sum1_out, sum1_in, sum1_send, sum1_recv)
    for copy in sum1:
        copy.start()

    n2 = 2 * clusters
    spread([u_t])
    terms = product(4, far_chunks, 0, far_f32, far_hi, far_lo, acc_far, n2, False)
    far2 = far_copies(far2_out, far2_in, far2_send, far2_recv)
    for h in range(4):
        far2_out[h] = fold(fold(terms[h * width:(h + 1) * width, :shared]))
        far2[h].start()
    terms = product(OWN, own_chunks, far_chunks, own_f32, own_hi, own_lo, acc_own, n2, False)
    image = collect(terms, 1)

    for copy in lam_copies:
        copy.wait_recv()
    lam = jnp.zeros((md * n_mode, 128), F32)
    part_row = lax.broadcasted_iota(jnp.int32, (md * n_mode, 128), 0) // md
    for d in range(n_mode):
        own = lax.rem(my_mode + n_mode - d, n_mode)
        tiled = jnp.concatenate([lam_buf[d][:md]] * n_mode, axis=0)
        lam = jnp.where(part_row == own, tiled, lam)
    t = column_of(basis_ref[0:1, :])
    t2 = t * t

    for copy in sum1:
        copy.wait_recv()
    sums = sum1_out[...]
    for d in range(n_dom - 1):
        sums = sums + sum1_in[d]
    sums = jnp.broadcast_to(jnp.sum(sums, axis=1, keepdims=True), (8, 128))
    rr0 = t2 * sums[0:1]
    alpha = rr0 / (t2 * (sums[1:2] + lam * sums[2:3]))
    alpha_lam = alpha * lam

    for h in range(4):
        far2[h].wait_recv()
    arrived = unfold(unfold(far2_in[0] + far2_in[1] + far2_in[2] + far2_in[3]))
    p_v = fold(image + widen(arrived))

    squares, curves = [], []
    for k in range(md * n_mode):
        a, al = alpha[k:k + 1], alpha_lam[k:k + 1]
        r = f_v - a * u_v - al * w_v
        image_r = u_v - a * p_v - al * q_v + lam[k:k + 1] * (m_v * r)
        squares.append(over(r * r))
        curves.append(over(r * image_r))
    sum2_out[...] = jnp.concatenate(squares + curves, axis=0)
    sum2 = sum_copies(sum2_out, sum2_in, sum2_send, sum2_recv)
    for copy in sum2:
        copy.start()

    u_nat = back(u_t)
    rows = [column_of(basis_ref[pl.ds(my_mode * levels + level, 1), :]) for level in range(levels)]

    for copy in sum2:
        copy.wait_recv()
    sums = sum2_out[...]
    for d in range(n_dom - 1):
        sums = sums + sum2_in[d]
    modes = md * n_mode
    sums = jnp.broadcast_to(jnp.sum(sums, axis=1, keepdims=True), (2 * modes, 128))
    rr1 = t2 * sums[:modes]
    beta = rr1 / rr0
    alpha1 = rr1 / (t2 * sums[modes:] - beta * (rr1 / alpha))
    coef_f = t * (alpha + alpha1 * (1.0 + beta))
    coef_u = -t * (alpha1 * alpha)
    coef_w = coef_u * lam
    for level in range(levels):
        c_f, c_u, c_w = (over(rows[level] * c) for c in (coef_f, coef_u, coef_w))
        out_ref[:, level, :] = c_f * f_nat + c_u * u_nat + c_w * w_nat

    for copy in lam_copies + far1 + far2 + sum1 + sum2:
        copy.wait_send()


def solution(mesh):
    n_dom, n_mode = mesh.shape["dom"], mesh.shape["mode"]

    def body(source, mass, lambdas, trace_basis, blocks, columns):
        slots, width, vertices = blocks.shape
        clusters = columns.shape[0]
        shared = clusters // 2
        md = lambdas.shape[0]
        levels = LEVELS // n_mode
        lines = vertices // 128
        vmem = pl.BlockSpec(memory_space=pltpu.VMEM)
        hbm = pl.BlockSpec(memory_space=pltpu.HBM)
        dma = pltpu.SemaphoreType.DMA
        chunks = vertices // 1024 + shared * width // 1024
        result = pl.pallas_call(
            functools.partial(kernel, n_dom, n_mode),
            out_shape=jax.ShapeDtypeStruct((lines, levels, 128), F32),
            in_specs=[hbm] * 6,
            out_specs=vmem,
            scratch_shapes=[
                pltpu.VMEM((lines, 128), F32),
                pltpu.VMEM((lines, 128), F32),
                pltpu.VMEM((1, md), F32),
                pltpu.VMEM(trace_basis.shape, F32),
                pltpu.VMEM((slots, clusters), jnp.int32),
                pltpu.VMEM((OWN, width, vertices), F32),
                pltpu.VMEM((slots - OWN, width, shared * width), F32),
                pltpu.VMEM((OWN * width, vertices), BF16),
                pltpu.VMEM((OWN * width, vertices), BF16),
                pltpu.VMEM(((slots - OWN) * width, shared * width), BF16),
                pltpu.VMEM(((slots - OWN) * width, shared * width), BF16),
                pltpu.VMEM((vertices, 4 * clusters), BF16),
                pltpu.VMEM((OWN * width, 4 * clusters), F32),
                pltpu.VMEM(((slots - OWN) * width, 4 * clusters), F32),
                pltpu.VMEM((n_mode, 8, 128), F32),
                pltpu.VMEM((4, width // 2, 2 * clusters), F32),
                pltpu.VMEM((4, width // 2, 2 * clusters), F32),
                pltpu.VMEM((4, width // 4, 4 * shared), F32),
                pltpu.VMEM((4, width // 4, 4 * shared), F32),
                pltpu.VMEM((8, 128), F32),
                pltpu.VMEM((n_dom - 1, 8, 128), F32),
                pltpu.VMEM((2 * md * n_mode, 128), F32),
                pltpu.VMEM((n_dom - 1, 2 * md * n_mode, 128), F32),
                dma((5,)),
                dma((chunks,)),
                dma((n_mode,)), dma((n_mode,)),
                dma((4,)), dma((4,)), dma((4,)), dma((4,)),
                dma((n_dom - 1,)), dma((n_dom - 1,)), dma((n_dom - 1,)), dma((n_dom - 1,)),
            ],
            compiler_params=pltpu.CompilerParams(
                collective_id=0, has_side_effects=True, vmem_limit_bytes=64 * 1024 * 1024),
        )(
            source.reshape(lines, 128), mass.reshape(lines, 128), lambdas.reshape(1, md),
            trace_basis, blocks, columns.T,
        )
        return jnp.transpose(result, (1, 0, 2)).reshape(levels, vertices)

    in_specs = (P("dom"), P("dom"), P("mode"), P(), P(None, None, "dom"), P("dom", None))
    return jax.shard_map(body, mesh=mesh, in_specs=in_specs, out_specs=P("mode", "dom"), check_vma=False)
```

```python
import functools

import jax
import jax.numpy as jnp
from jax import lax
from jax.experimental import pallas as pl
from jax.experimental.pallas import tpu as pltpu
from jax.sharding import PartitionSpec as P

LEVELS = 16
OFFSETS = (-2, -1, 1, 2)
OWN = 5
HIGHEST = lax.Precision.HIGHEST
MESH = pl.DeviceIdType.MESH
F32 = jnp.float32
BF16 = jnp.bfloat16


def halves(value):
    high = value.astype(BF16)
    return high, (value - high.astype(F32)).astype(BF16)


def dot(a, b, dims=((1,), (0,)), precision=None):
    return lax.dot_general(a, b, (dims, ((), ())), precision=precision, preferred_element_type=F32)


def fold(value):
    half = value.shape[0] // 2
    return jnp.concatenate([value[:half], value[half:]], axis=1)


def unfold(value):
    half = value.shape[1] // 2
    return jnp.concatenate([value[:, :half], value[:, half:]], axis=0)


def row_of(column):
    n = column.shape[0]
    eye = lax.broadcasted_iota(jnp.int32, (n, n), 0) == lax.broadcasted_iota(jnp.int32, (n, n), 1)
    return jnp.sum(jnp.where(eye, jnp.broadcast_to(column[:, 0:1], (n, n)), 0.0), axis=0, keepdims=True)


def column_of(row):
    n = row.shape[1]
    eye = lax.broadcasted_iota(jnp.int32, (n, n), 0) == lax.broadcasted_iota(jnp.int32, (n, n), 1)
    spread = jnp.where(eye, jnp.broadcast_to(row, (n, n)), 0.0)
    return jnp.broadcast_to(jnp.sum(spread, axis=1, keepdims=True), (n, 128))


def kernel(
    n_dom, n_mode,
    source_hbm, mass_hbm, lam_hbm, basis_hbm, blocks_ref, cols_hbm, out_ref,
    source_ref, mass_ref, lam_ref, basis_ref, cols_ref,
    own_f32, far_f32, own_hi, own_lo, far_hi, far_lo, v_ref, acc_own, acc_far,
    lam_buf, far1_out, far1_in, far2_out, far2_in, sum1_out, sum1_in, sum2_out, sum2_in,
    small_sem, load_sem, lam_send, lam_recv, far1_send, far1_recv, far2_send, far2_recv,
    sum1_send, sum1_recv, sum2_send, sum2_recv,
):
    me = lax.axis_index("dom")
    my_mode = lax.axis_index("mode")
    width = own_f32.shape[1]
    clusters = cols_ref.shape[1]
    shared = clusters // 2
    md = lam_ref.shape[1]
    levels = out_ref.shape[1]
    span = 1024
    modes = md * n_mode
    far_chunks = shared * width // span
    own_chunks = clusters * width // span
    per_chunk = span // width

    small = [
        pltpu.make_async_copy(src, dst, small_sem.at[n])
        for n, (src, dst) in enumerate((
            (source_hbm, source_ref), (mass_hbm, mass_ref), (lam_hbm, lam_ref),
            (basis_hbm, basis_ref), (cols_hbm, cols_ref)))
    ]
    for copy in small:
        copy.start()
    loads = []
    for n in range(far_chunks):
        lanes = pl.ds(n * span, span)
        loads.append(pltpu.make_async_copy(
            blocks_ref.at[pl.ds(OWN, 4), :, lanes], far_f32.at[:, :, lanes], load_sem.at[n]))
    for n in range(own_chunks):
        lanes = pl.ds(n * span, span)
        loads.append(pltpu.make_async_copy(
            blocks_ref.at[pl.ds(0, OWN), :, lanes], own_f32.at[:, :, lanes], load_sem.at[far_chunks + n]))
    for load in loads:
        load.start()

    barrier = pltpu.get_barrier_semaphore()
    for d in range(1, n_mode):
        pl.semaphore_signal(barrier, inc=1, device_id=(me, lax.rem(my_mode + d, n_mode)), device_id_type=MESH)
    for d in range(1, n_dom):
        pl.semaphore_signal(barrier, inc=1, device_id=(lax.rem(me + d, n_dom), my_mode), device_id_type=MESH)

    for copy in small:
        copy.wait()
    f_nat = mass_ref[...] * source_ref[...]
    m_nat = mass_ref[...]
    w_nat = m_nat * f_nat
    pairs = clusters // 2
    pair_row = lax.broadcasted_iota(jnp.int32, (pairs, clusters), 0)
    cluster_col = lax.broadcasted_iota(jnp.int32, (pairs, clusters), 1)
    even = (cluster_col == 2 * pair_row).astype(F32)
    odd = (cluster_col == 2 * pair_row + 1).astype(F32)

    def across(nat):
        first = dot(nat, even, ((0,), (0,)), HIGHEST)
        second = dot(nat, odd, ((0,), (0,)), HIGHEST)
        return first[:width] + second[width:]

    def back(vec):
        first = dot(even, vec, ((1,), (1,)), HIGHEST)
        second = dot(odd, vec, ((1,), (1,)), HIGHEST)
        return jnp.concatenate([first, second], axis=1)

    m_t = across(m_nat)
    f_t = across(f_nat)
    w_t = m_t * f_t

    def spread(vectors, first, last):
        high = [v.astype(BF16).astype(F32) for v in vectors]
        packed = jnp.concatenate(high + [v - h for v, h in zip(vectors, high)], axis=1)
        lane = lax.rem(lax.broadcasted_iota(jnp.int32, packed.shape, 1), clusters)
        n = packed.shape[1]

        def place(g, carry):
            v_ref[pl.ds(pl.multiple_of(g * width, width), width), 0:n] = jnp.where(lane == g, packed, 0.0).astype(BF16)
            return carry
        lax.fori_loop(first, last, place, 0, unroll=8)

    spread([f_t, w_t], 0, clusters)

    lam_row = lam_ref[...]
    lam_tile = jnp.concatenate([column_of(lam_row), jnp.zeros((8 - md, 128), F32)], axis=0)
    lam_buf[0] = lam_tile
    def far_copies(out_buf, in_buf, send, recv):
        copies = []
        for h, offset in enumerate(OFFSETS):
            copies.append(pltpu.make_async_remote_copy(
                src_ref=out_buf.at[h], dst_ref=in_buf.at[h], send_sem=send.at[h], recv_sem=recv.at[h],
                device_id=(lax.rem(me + n_dom + offset, n_dom), my_mode), device_id_type=MESH))
        return copies

    def sum_copies(out_buf, in_buf, send, recv):
        copies = []
        for d in range(1, n_dom):
            copies.append(pltpu.make_async_remote_copy(
                src_ref=out_buf, dst_ref=in_buf.at[d - 1], send_sem=send.at[d - 1], recv_sem=recv.at[d - 1],
                device_id=(lax.rem(me + d, n_dom), my_mode), device_id_type=MESH))
        return copies

    def product(count, chunks, first_load, full, high, low, acc, n, first_pass):
        for c in range(chunks):
            lanes = pl.ds(c * span, span)
            if first_pass:
                loads[first_load + c].wait()
                hi, lo = halves(full[:, :, lanes].reshape(count * width, span))
                high[:, lanes] = hi
                low[:, lanes] = lo
            else:
                hi, lo = high[:, lanes], low[:, lanes]
            right = v_ref[lanes, 0:n]
            part = dot(hi, right) + dot(lo, right)
            if c:
                acc[:, 0:n] += part
            else:
                acc[:, 0:n] = part
        return acc[:, 0:n // 2] + acc[:, n // 2:n]

    cluster_row = lax.broadcasted_iota(jnp.int32, (clusters, clusters), 0)

    def collect(terms, vectors):
        total = terms[:width]
        high, low = halves(terms[width:])
        moved = None
        for s in range(1, OWN):
            hot = (cols_ref[s:s + 1, :] == cluster_row).astype(F32).astype(BF16)
            if vectors == 2:
                zero = jnp.zeros_like(hot)
                hot = jnp.concatenate([jnp.concatenate([hot, zero], 1), jnp.concatenate([zero, hot], 1)], 0)
            rows = slice((s - 1) * width, s * width)
            part = dot(high[rows], hot, ((1,), (1,))) + dot(low[rows], hot, ((1,), (1,)))
            moved = part if moved is None else moved + part
        return total + moved

    def widen(value):
        return jnp.concatenate([value, jnp.zeros((width, clusters - shared), F32)], axis=1)

    n1 = 4 * clusters
    terms = product(4, far_chunks, 0, far_f32, far_hi, far_lo, acc_far, n1, True)
    far1 = far_copies(far1_out, far1_in, far1_send, far1_recv)
    for h in range(4):
        rows = terms[h * width:(h + 1) * width]
        both = jnp.concatenate([rows[:, :shared], rows[:, clusters:clusters + shared]], axis=1)
        far1_out[h] = fold(both)
    wait_for = n_dom - 1 + n_mode - 1
    pl.semaphore_wait(barrier, wait_for)
    for copy in far1:
        copy.start()
    lam_copies = []
    for d in range(1, n_mode):
        copy = pltpu.make_async_remote_copy(
            src_ref=lam_buf.at[0], dst_ref=lam_buf.at[d], send_sem=lam_send.at[d], recv_sem=lam_recv.at[d],
            device_id=(me, lax.rem(my_mode + d, n_mode)), device_id_type=MESH)
        copy.start()
        lam_copies.append(copy)
    terms = product(OWN, own_chunks, far_chunks, own_f32, own_hi, own_lo, acc_own, n1, True)
    image = collect(terms, 2)
    for h in range(4):
        far1[h].wait_recv()
    arrived = unfold(far1_in[0] + far1_in[1] + far1_in[2] + far1_in[3])
    u_t = image[:, :clusters] + widen(arrived[:, :shared])
    q_t = image[:, clusters:] + widen(arrived[:, shared:])

    n2 = 2 * clusters
    spread([u_t], 0, shared)
    terms = product(4, far_chunks, 0, far_f32, far_hi, far_lo, acc_far, n2, False)
    far2 = far_copies(far2_out, far2_in, far2_send, far2_recv)
    for h in range(4):
        far2_out[h] = fold(fold(terms[h * width:(h + 1) * width, :shared]))
        far2[h].start()

    f_v, w_v, m_v, u_v, q_v = fold(f_t), fold(w_t), fold(m_t), fold(u_t), fold(q_t)

    def over(value):
        return jnp.sum(value, axis=0, keepdims=True)

    sum1_out[...] = jnp.concatenate(
        [over(f_v * f_v), over(f_v * u_v), over(f_v * w_v), jnp.zeros((5, 128), F32)], axis=0)
    sum1 = sum_copies(sum1_out, sum1_in, sum1_send, sum1_recv)
    for copy in sum1:
        copy.start()

    spread([u_t], shared, clusters)
    terms = product(OWN, own_chunks, far_chunks, own_f32, own_hi, own_lo, acc_own, n2, False)
    image = collect(terms, 1)

    for copy in lam_copies:
        copy.wait_recv()
    lam = jnp.zeros((md * n_mode, 128), F32)
    part_row = lax.broadcasted_iota(jnp.int32, (md * n_mode, 128), 0) // md
    for d in range(n_mode):
        own = lax.rem(my_mode + n_mode - d, n_mode)
        tiled = jnp.concatenate([lam_buf[d][:md]] * n_mode, axis=0)
        lam = jnp.where(part_row == own, tiled, lam)
    t = column_of(basis_ref[0:1, :])
    t2 = t * t

    for copy in sum1:
        copy.wait_recv()
    sums = sum1_out[...]
    for d in range(n_dom - 1):
        sums = sums + sum1_in[d]
    sums = jnp.broadcast_to(jnp.sum(sums, axis=1, keepdims=True), (8, 128))
    rr0 = t2 * sums[0:1]
    alpha = rr0 / (t2 * (sums[1:2] + lam * sums[2:3]))
    alpha_lam = alpha * lam

    for h in range(4):
        far2[h].wait_recv()
    arrived = unfold(unfold(far2_in[0] + far2_in[1] + far2_in[2] + far2_in[3]))
    p_v = fold(image + widen(arrived))

    squares, curves = [], []
    for k in range(md * n_mode):
        a, al = alpha[k:k + 1], alpha_lam[k:k + 1]
        r = f_v - a * u_v - al * w_v
        image_r = u_v - a * p_v - al * q_v + lam[k:k + 1] * (m_v * r)
        squares.append(over(r * r))
        curves.append(over(r * image_r))
    sum2_out[...] = jnp.zeros((8, 128), F32)
    for row, parts in enumerate((squares, curves)):
        column = jnp.sum(jnp.concatenate(parts, axis=0), axis=1, keepdims=True)
        sum2_out[row:row + 1, 0:modes] = row_of(column)
    sum2 = sum_copies(sum2_out, sum2_in, sum2_send, sum2_recv)
    for copy in sum2:
        copy.start()

    u_nat = back(u_t)
    basis_own = jnp.concatenate(
        [basis_ref[pl.ds(my_mode * levels + level, 1), :] for level in range(levels)], axis=0)
    t_row = basis_ref[0:1, :]
    t2_row = t_row * t_row
    alpha_row, rr0_row, lam_row = row_of(alpha), row_of(rr0), row_of(lam)

    for copy in sum2:
        copy.wait_recv()
    sums = sum2_out[...]
    for d in range(n_dom - 1):
        sums = sums + sum2_in[d]
    rr1 = t2_row * sums[0:1, 0:modes]
    beta = rr1 / rr0_row
    alpha1 = rr1 / (t2_row * sums[1:2, 0:modes] - beta * (rr1 / alpha_row))
    coef_f = t_row * (alpha_row + alpha1 * (1.0 + beta))
    coef_u = -t_row * (alpha1 * alpha_row)
    coef_w = coef_u * lam_row
    c_f, c_u, c_w = (
        jnp.broadcast_to(jnp.sum(basis_own * c, axis=1, keepdims=True), (levels, 128))
        for c in (coef_f, coef_u, coef_w))
    for level in range(levels):
        one = slice(level, level + 1)
        out_ref[:, level, :] = c_f[one] * f_nat + c_u[one] * u_nat + c_w[one] * w_nat

    for copy in lam_copies + far1 + far2 + sum1 + sum2:
        copy.wait_send()


def solution(mesh):
    n_dom, n_mode = mesh.shape["dom"], mesh.shape["mode"]

    def body(source, mass, lambdas, trace_basis, blocks, columns):
        slots, width, vertices = blocks.shape
        clusters = columns.shape[0]
        shared = clusters // 2
        md = lambdas.shape[0]
        levels = LEVELS // n_mode
        lines = vertices // 128
        vmem = pl.BlockSpec(memory_space=pltpu.VMEM)
        hbm = pl.BlockSpec(memory_space=pltpu.HBM)
        dma = pltpu.SemaphoreType.DMA
        chunks = vertices // 1024 + shared * width // 1024
        result = pl.pallas_call(
            functools.partial(kernel, n_dom, n_mode),
            out_shape=jax.ShapeDtypeStruct((lines, levels, 128), F32),
            in_specs=[hbm] * 6,
            out_specs=vmem,
            scratch_shapes=[
                pltpu.VMEM((lines, 128), F32),
                pltpu.VMEM((lines, 128), F32),
                pltpu.VMEM((1, md), F32),
                pltpu.VMEM(trace_basis.shape, F32),
                pltpu.VMEM((slots, clusters), jnp.int32),
                pltpu.VMEM((OWN, width, vertices), F32),
                pltpu.VMEM((slots - OWN, width, shared * width), F32),
                pltpu.VMEM((OWN * width, vertices), BF16),
                pltpu.VMEM((OWN * width, vertices), BF16),
                pltpu.VMEM(((slots - OWN) * width, shared * width), BF16),
                pltpu.VMEM(((slots - OWN) * width, shared * width), BF16),
                pltpu.VMEM((vertices, 4 * clusters), BF16),
                pltpu.VMEM((OWN * width, 4 * clusters), F32),
                pltpu.VMEM(((slots - OWN) * width, 4 * clusters), F32),
                pltpu.VMEM((n_mode, 8, 128), F32),
                pltpu.VMEM((4, width // 2, 2 * clusters), F32),
                pltpu.VMEM((4, width // 2, 2 * clusters), F32),
                pltpu.VMEM((4, width // 4, 4 * shared), F32),
                pltpu.VMEM((4, width // 4, 4 * shared), F32),
                pltpu.VMEM((8, 128), F32),
                pltpu.VMEM((n_dom - 1, 8, 128), F32),
                pltpu.VMEM((8, 128), F32),
                pltpu.VMEM((n_dom - 1, 8, 128), F32),
                dma((5,)),
                dma((chunks,)),
                dma((n_mode,)), dma((n_mode,)),
                dma((4,)), dma((4,)), dma((4,)), dma((4,)),
                dma((n_dom - 1,)), dma((n_dom - 1,)), dma((n_dom - 1,)), dma((n_dom - 1,)),
            ],
            compiler_params=pltpu.CompilerParams(
                collective_id=0, has_side_effects=True, vmem_limit_bytes=64 * 1024 * 1024 - 131072),
        )(
            source.reshape(lines, 128), mass.reshape(lines, 128), lambdas.reshape(1, md),
            trace_basis, blocks, columns.T,
        )
        return jnp.transpose(result, (1, 0, 2)).reshape(levels, vertices)

    in_specs = (P("dom"), P("dom"), P("mode"), P(), P(None, None, "dom"), P("dom", None))
    return jax.shard_map(body, mesh=mesh, in_specs=in_specs, out_specs=P("mode", "dom"), check_vma=False)
```

```python
import functools

import jax
import jax.numpy as jnp
from jax import lax
from jax.experimental import pallas as pl
from jax.experimental.pallas import tpu as pltpu
from jax.sharding import PartitionSpec as P

LEVELS = 16
OFFSETS = (-2, -1, 1, 2)
OWN = 5
HIGHEST = lax.Precision.HIGHEST
MESH = pl.DeviceIdType.MESH
F32 = jnp.float32
BF16 = jnp.bfloat16


def halves(value):
    high = value.astype(BF16)
    return high, (value - high.astype(F32)).astype(BF16)


def dot(a, b, dims=((1,), (0,)), precision=None):
    return lax.dot_general(a, b, (dims, ((), ())), precision=precision, preferred_element_type=F32)


def fold(value):
    half = value.shape[0] // 2
    return jnp.concatenate([value[:half], value[half:]], axis=1)


def unfold(value):
    half = value.shape[1] // 2
    return jnp.concatenate([value[:, :half], value[:, half:]], axis=0)


def row_of(column):
    n = column.shape[0]
    eye = lax.broadcasted_iota(jnp.int32, (n, n), 0) == lax.broadcasted_iota(jnp.int32, (n, n), 1)
    return jnp.sum(jnp.where(eye, jnp.broadcast_to(column[:, 0:1], (n, n)), 0.0), axis=0, keepdims=True)


def column_of(row):
    n = row.shape[1]
    eye = lax.broadcasted_iota(jnp.int32, (n, n), 0) == lax.broadcasted_iota(jnp.int32, (n, n), 1)
    spread = jnp.where(eye, jnp.broadcast_to(row, (n, n)), 0.0)
    return jnp.broadcast_to(jnp.sum(spread, axis=1, keepdims=True), (n, 128))


def kernel(
    n_dom, n_mode,
    source_hbm, mass_hbm, lam_hbm, basis_hbm, blocks_ref, cols_hbm, out_ref,
    source_ref, mass_ref, lam_ref, basis_ref, cols_ref,
    own_f32, far_f32, own_hi, own_lo, far_hi, far_lo, v_ref, acc_own, acc_far,
    lam_buf, far1_out, far1_in, far2_out, far2_in, sum1_out, sum1_in, sum2_out, sum2_in,
    small_sem, load_sem, lam_send, lam_recv, far1_send, far1_recv, far2_send, far2_recv,
    sum1_send, sum1_recv, sum2_send, sum2_recv,
):
    me = lax.axis_index("dom")
    my_mode = lax.axis_index("mode")
    width = own_f32.shape[1]
    clusters = cols_ref.shape[1]
    shared = clusters // 2
    md = lam_ref.shape[1]
    levels = out_ref.shape[1]
    span = 1024
    modes = md * n_mode
    far_chunks = shared * width // span
    own_chunks = clusters * width // span
    per_chunk = span // width

    small = [
        pltpu.make_async_copy(src, dst, small_sem.at[n])
        for n, (src, dst) in enumerate((
            (source_hbm, source_ref), (mass_hbm, mass_ref), (lam_hbm, lam_ref),
            (basis_hbm, basis_ref), (cols_hbm, cols_ref)))
    ]
    for copy in small:
        copy.start()
    loads = []
    for n in range(far_chunks):
        lanes = pl.ds(n * span, span)
        loads.append(pltpu.make_async_copy(
            blocks_ref.at[pl.ds(OWN, 4), :, lanes], far_f32.at[:, :, lanes], load_sem.at[n]))
    for n in range(own_chunks):
        lanes = pl.ds(n * span, span)
        loads.append(pltpu.make_async_copy(
            blocks_ref.at[pl.ds(0, OWN), :, lanes], own_f32.at[:, :, lanes], load_sem.at[far_chunks + n]))
    for load in loads:
        load.start()

    barrier = pltpu.get_barrier_semaphore()
    for d in range(1, n_mode):
        pl.semaphore_signal(barrier, inc=1, device_id=(me, lax.rem(my_mode + d, n_mode)), device_id_type=MESH)
    for d in range(1, n_dom):
        pl.semaphore_signal(barrier, inc=1, device_id=(lax.rem(me + d, n_dom), my_mode), device_id_type=MESH)

    for copy in small:
        copy.wait()
    f_nat = mass_ref[...] * source_ref[...]
    m_nat = mass_ref[...]
    w_nat = m_nat * f_nat
    pairs = clusters // 2
    pair_row = lax.broadcasted_iota(jnp.int32, (pairs, clusters), 0)
    cluster_col = lax.broadcasted_iota(jnp.int32, (pairs, clusters), 1)
    even = (cluster_col == 2 * pair_row).astype(F32)
    odd = (cluster_col == 2 * pair_row + 1).astype(F32)

    def across(nat):
        first = dot(nat, even, ((0,), (0,)), HIGHEST)
        second = dot(nat, odd, ((0,), (0,)), HIGHEST)
        return first[:width] + second[width:]

    def back(vec):
        first = dot(even, vec, ((1,), (1,)), HIGHEST)
        second = dot(odd, vec, ((1,), (1,)), HIGHEST)
        return jnp.concatenate([first, second], axis=1)

    m_t = across(m_nat)
    f_t = across(f_nat)
    w_t = m_t * f_t

    def spread(vectors, first, last):
        high = [v.astype(BF16).astype(F32) for v in vectors]
        packed = jnp.concatenate(high + [v - h for v, h in zip(vectors, high)], axis=1)
        lane = lax.rem(lax.broadcasted_iota(jnp.int32, packed.shape, 1), clusters)
        n = packed.shape[1]

        def place(g, carry):
            v_ref[pl.ds(pl.multiple_of(g * width, width), width), 0:n] = jnp.where(lane == g, packed, 0.0).astype(BF16)
            return carry
        lax.fori_loop(first, last, place, 0, unroll=8)

    spread([f_t, w_t], 0, clusters)

    lam_row = lam_ref[...]
    lam_tile = jnp.concatenate([column_of(lam_row), jnp.zeros((8 - md, 128), F32)], axis=0)
    lam_buf[0] = lam_tile
    def far_copies(out_buf, in_buf, send, recv):
        copies = []
        for h, offset in enumerate(OFFSETS):
            copies.append(pltpu.make_async_remote_copy(
                src_ref=out_buf.at[h], dst_ref=in_buf.at[h], send_sem=send.at[h], recv_sem=recv.at[h],
                device_id=(lax.rem(me + n_dom + offset, n_dom), my_mode), device_id_type=MESH))
        return copies

    def sum_copies(out_buf, in_buf, send, recv):
        copies = []
        for d in range(1, n_dom):
            copies.append(pltpu.make_async_remote_copy(
                src_ref=out_buf, dst_ref=in_buf.at[d - 1], send_sem=send.at[d - 1], recv_sem=recv.at[d - 1],
                device_id=(lax.rem(me + d, n_dom), my_mode), device_id_type=MESH))
        return copies

    def product(count, chunks, first_load, full, high, low, acc, n, first_pass):
        for c in range(chunks):
            lanes = pl.ds(c * span, span)
            if first_pass:
                loads[first_load + c].wait()
                hi, lo = halves(full[:, :, lanes].reshape(count * width, span))
                high[:, lanes] = hi
                low[:, lanes] = lo
            else:
                hi, lo = high[:, lanes], low[:, lanes]
            right = v_ref[lanes, 0:n]
            part = dot(hi, right) + dot(lo, right)
            if c:
                acc[:, 0:n] += part
            else:
                acc[:, 0:n] = part
        return acc[:, 0:n // 2] + acc[:, n // 2:n]

    cluster_row = lax.broadcasted_iota(jnp.int32, (clusters, clusters), 0)

    def collect(terms, vectors):
        total = terms[:width]
        high, low = halves(terms[width:])
        moved = None
        for s in range(1, OWN):
            hot = (cols_ref[s:s + 1, :] == cluster_row).astype(F32).astype(BF16)
            if vectors == 2:
                zero = jnp.zeros_like(hot)
                hot = jnp.concatenate([jnp.concatenate([hot, zero], 1), jnp.concatenate([zero, hot], 1)], 0)
            rows = slice((s - 1) * width, s * width)
            part = dot(high[rows], hot, ((1,), (1,))) + dot(low[rows], hot, ((1,), (1,)))
            moved = part if moved is None else moved + part
        return total + moved

    def widen(value):
        return jnp.concatenate([value, jnp.zeros((width, clusters - shared), F32)], axis=1)

    n1 = 4 * clusters
    terms = product(4, far_chunks, 0, far_f32, far_hi, far_lo, acc_far, n1, True)
    far1 = far_copies(far1_out, far1_in, far1_send, far1_recv)
    for h in range(4):
        rows = terms[h * width:(h + 1) * width]
        both = jnp.concatenate([rows[:, :shared], rows[:, clusters:clusters + shared]], axis=1)
        far1_out[h] = fold(both)
    wait_for = n_dom - 1 + n_mode - 1
    pl.semaphore_wait(barrier, wait_for)
    for copy in far1:
        copy.start()
    lam_copies = []
    for d in range(1, n_mode):
        copy = pltpu.make_async_remote_copy(
            src_ref=lam_buf.at[0], dst_ref=lam_buf.at[d], send_sem=lam_send.at[d], recv_sem=lam_recv.at[d],
            device_id=(me, lax.rem(my_mode + d, n_mode)), device_id_type=MESH)
        copy.start()
        lam_copies.append(copy)
    terms = product(OWN, own_chunks, far_chunks, own_f32, own_hi, own_lo, acc_own, n1, True)
    image = collect(terms, 2)
    for h in range(4):
        far1[h].wait_recv()
    arrived = unfold(far1_in[0] + far1_in[1] + far1_in[2] + far1_in[3])
    u_t = image[:, :clusters] + widen(arrived[:, :shared])
    q_t = image[:, clusters:] + widen(arrived[:, shared:])

    n2 = 2 * clusters
    spread([u_t], 0, shared)
    terms = product(4, far_chunks, 0, far_f32, far_hi, far_lo, acc_far, n2, False)
    far2 = far_copies(far2_out, far2_in, far2_send, far2_recv)
    for h in range(4):
        far2_out[h] = fold(fold(terms[h * width:(h + 1) * width, :shared]))
        far2[h].start()

    f_v, w_v, m_v, u_v, q_v = fold(f_t), fold(w_t), fold(m_t), fold(u_t), fold(q_t)

    def over(value):
        return jnp.sum(value, axis=0, keepdims=True)

    sum1_out[...] = jnp.concatenate(
        [over(f_v * f_v), over(f_v * u_v), over(f_v * w_v), jnp.zeros((5, 128), F32)], axis=0)
    sum1 = sum_copies(sum1_out, sum1_in, sum1_send, sum1_recv)
    for copy in sum1:
        copy.start()

    spread([u_t], shared, clusters)
    terms = product(OWN, own_chunks, far_chunks, own_f32, own_hi, own_lo, acc_own, n2, False)
    image = collect(terms, 1)

    for copy in lam_copies:
        copy.wait_recv()
    lam = jnp.zeros((md * n_mode, 128), F32)
    part_row = lax.broadcasted_iota(jnp.int32, (md * n_mode, 128), 0) // md
    for d in range(n_mode):
        own = lax.rem(my_mode + n_mode - d, n_mode)
        tiled = jnp.concatenate([lam_buf[d][:md]] * n_mode, axis=0)
        lam = jnp.where(part_row == own, tiled, lam)
    t = column_of(basis_ref[0:1, :])
    t2 = t * t

    for copy in sum1:
        copy.wait_recv()
    sums = sum1_out[...]
    for d in range(n_dom - 1):
        sums = sums + sum1_in[d]
    sums = jnp.broadcast_to(jnp.sum(sums, axis=1, keepdims=True), (8, 128))
    rr0 = t2 * sums[0:1]
    alpha = rr0 / (t2 * (sums[1:2] + lam * sums[2:3]))
    alpha_lam = alpha * lam

    for h in range(4):
        far2[h].wait_recv()
    arrived = unfold(unfold(far2_in[0] + far2_in[1] + far2_in[2] + far2_in[3]))
    p_v = fold(image + widen(arrived))

    squares, curves = [], []
    for k in range(md * n_mode):
        a, al = alpha[k:k + 1], alpha_lam[k:k + 1]
        r = f_v - a * u_v - al * w_v
        image_r = u_v - a * p_v - al * q_v + lam[k:k + 1] * (m_v * r)
        squares.append(over(r * r))
        curves.append(over(r * image_r))
    sum2_out[...] = jnp.zeros((8, 128), F32)
    for row, parts in enumerate((squares, curves)):
        column = jnp.sum(jnp.concatenate(parts, axis=0), axis=1, keepdims=True)
        sum2_out[row:row + 1, 0:modes] = row_of(column)
    sum2 = sum_copies(sum2_out, sum2_in, sum2_send, sum2_recv)
    for copy in sum2:
        copy.start()

    u_nat = back(u_t)
    basis_own = jnp.concatenate(
        [basis_ref[pl.ds(my_mode * levels + level, 1), :] for level in range(levels)], axis=0)
    t_row = basis_ref[0:1, :]
    t2_row = t_row * t_row
    alpha_row, rr0_row, lam_row = row_of(alpha), row_of(rr0), row_of(lam)

    for copy in sum2:
        copy.wait_recv()
    sums = sum2_out[...]
    for d in range(n_dom - 1):
        sums = sums + sum2_in[d]
    rr1 = t2_row * sums[0:1, 0:modes]
    beta = rr1 / rr0_row
    alpha1 = rr1 / (t2_row * sums[1:2, 0:modes] - beta * (rr1 / alpha_row))
    coef_f = t_row * (alpha_row + alpha1 * (1.0 + beta))
    coef_u = -t_row * (alpha1 * alpha_row)
    coef_w = coef_u * lam_row
    c_f, c_u, c_w = (
        jnp.broadcast_to(jnp.sum(basis_own * c, axis=1, keepdims=True), (levels, 128))
        for c in (coef_f, coef_u, coef_w))
    for level in range(levels):
        one = slice(level, level + 1)
        out_ref[:, level, :] = c_f[one] * f_nat + c_u[one] * u_nat + c_w[one] * w_nat

    for copy in lam_copies + far1 + far2 + sum1 + sum2:
        copy.wait_send()


def solution(mesh):
    n_dom, n_mode = mesh.shape["dom"], mesh.shape["mode"]

    def body(source, mass, lambdas, trace_basis, blocks, columns):
        slots, width, vertices = blocks.shape
        clusters = columns.shape[0]
        shared = clusters // 2
        md = lambdas.shape[0]
        levels = LEVELS // n_mode
        lines = vertices // 128
        vmem = pl.BlockSpec(memory_space=pltpu.VMEM)
        hbm = pl.BlockSpec(memory_space=pltpu.HBM)
        dma = pltpu.SemaphoreType.DMA
        chunks = vertices // 1024 + shared * width // 1024
        result = pl.pallas_call(
            functools.partial(kernel, n_dom, n_mode),
            out_shape=pltpu.VMEM((lines, levels, 128), F32),
            in_specs=[hbm] * 6,
            out_specs=vmem,
            scratch_shapes=[
                pltpu.VMEM((lines, 128), F32),
                pltpu.VMEM((lines, 128), F32),
                pltpu.VMEM((1, md), F32),
                pltpu.VMEM(trace_basis.shape, F32),
                pltpu.VMEM((slots, clusters), jnp.int32),
                pltpu.VMEM((OWN, width, vertices), F32),
                pltpu.VMEM((slots - OWN, width, shared * width), F32),
                pltpu.VMEM((OWN * width, vertices), BF16),
                pltpu.VMEM((OWN * width, vertices), BF16),
                pltpu.VMEM(((slots - OWN) * width, shared * width), BF16),
                pltpu.VMEM(((slots - OWN) * width, shared * width), BF16),
                pltpu.VMEM((vertices, 4 * clusters), BF16),
                pltpu.VMEM((OWN * width, 4 * clusters), F32),
                pltpu.VMEM(((slots - OWN) * width, 4 * clusters), F32),
                pltpu.VMEM((n_mode, 8, 128), F32),
                pltpu.VMEM((4, width // 2, 2 * clusters), F32),
                pltpu.VMEM((4, width // 2, 2 * clusters), F32),
                pltpu.VMEM((4, width // 4, 4 * shared), F32),
                pltpu.VMEM((4, width // 4, 4 * shared), F32),
                pltpu.VMEM((8, 128), F32),
                pltpu.VMEM((n_dom - 1, 8, 128), F32),
                pltpu.VMEM((8, 128), F32),
                pltpu.VMEM((n_dom - 1, 8, 128), F32),
                dma((5,)),
                dma((chunks,)),
                dma((n_mode,)), dma((n_mode,)),
                dma((4,)), dma((4,)), dma((4,)), dma((4,)),
                dma((n_dom - 1,)), dma((n_dom - 1,)), dma((n_dom - 1,)), dma((n_dom - 1,)),
            ],
            compiler_params=pltpu.CompilerParams(
                collective_id=0, has_side_effects=True, vmem_limit_bytes=64 * 1024 * 1024 - 262144),
        )(
            source.reshape(lines, 128), mass.reshape(lines, 128), lambdas.reshape(1, md),
            trace_basis, blocks, columns.T,
        )
        return jnp.transpose(result, (1, 0, 2)).reshape(levels, vertices)

    in_specs = (P("dom"), P("dom"), P("mode"), P(), P(None, None, "dom"), P("dom", None))
    return jax.shard_map(body, mesh=mesh, in_specs=in_specs, out_specs=P("mode", "dom"), check_vma=False)
```

```python
import functools

import jax
import jax.numpy as jnp
from jax import lax
from jax.experimental import pallas as pl
from jax.experimental.pallas import tpu as pltpu
from jax.sharding import PartitionSpec as P

LEVELS = 16
OFFSETS = (-2, -1, 1, 2)
OWN = 5
HIGHEST = lax.Precision.HIGHEST
MESH = pl.DeviceIdType.MESH
F32 = jnp.float32
BF16 = jnp.bfloat16


def halves(value):
    high = value.astype(BF16)
    return high, (value - high.astype(F32)).astype(BF16)


def dot(a, b, dims=((1,), (0,)), precision=None):
    return lax.dot_general(a, b, (dims, ((), ())), precision=precision, preferred_element_type=F32)


def fold(value):
    half = value.shape[0] // 2
    return jnp.concatenate([value[:half], value[half:]], axis=1)


def unfold(value):
    half = value.shape[1] // 2
    return jnp.concatenate([value[:, :half], value[:, half:]], axis=0)


def row_of(column):
    n = column.shape[0]
    eye = lax.broadcasted_iota(jnp.int32, (n, n), 0) == lax.broadcasted_iota(jnp.int32, (n, n), 1)
    return jnp.sum(jnp.where(eye, jnp.broadcast_to(column[:, 0:1], (n, n)), 0.0), axis=0, keepdims=True)


def column_of(row):
    n = row.shape[1]
    eye = lax.broadcasted_iota(jnp.int32, (n, n), 0) == lax.broadcasted_iota(jnp.int32, (n, n), 1)
    spread = jnp.where(eye, jnp.broadcast_to(row, (n, n)), 0.0)
    return jnp.broadcast_to(jnp.sum(spread, axis=1, keepdims=True), (n, 128))


def kernel(
    n_dom, n_mode,
    source_hbm, mass_hbm, lam_hbm, basis_hbm, blocks_ref, cols_hbm, out_ref,
    source_ref, mass_ref, lam_ref, basis_ref, cols_ref,
    own_f32, far_f32, own_hi, own_lo, far_hi, far_lo, v_ref, acc_own, acc_far,
    lam_buf, far1_out, far1_in, far2_out, far2_in, sum1_out, sum1_in, sum2_out, sum2_in,
    small_sem, load_sem, lam_send, lam_recv, far1_send, far1_recv, far2_send, far2_recv,
    sum1_send, sum1_recv, sum2_send, sum2_recv,
):
    me = lax.axis_index("dom")
    my_mode = lax.axis_index("mode")
    width = own_f32.shape[1]
    clusters = cols_ref.shape[1]
    shared = clusters // 2
    md = lam_ref.shape[1]
    levels = out_ref.shape[1]
    span = 1024
    modes = md * n_mode
    far_chunks = shared * width // span
    own_chunks = clusters * width // span
    per_chunk = span // width

    small = [
        pltpu.make_async_copy(src, dst, small_sem.at[n])
        for n, (src, dst) in enumerate((
            (source_hbm, source_ref), (mass_hbm, mass_ref), (lam_hbm, lam_ref),
            (basis_hbm, basis_ref), (cols_hbm, cols_ref)))
    ]
    for copy in small:
        copy.start()
    loads = []
    for n in range(far_chunks):
        lanes = pl.ds(n * span, span)
        loads.append(pltpu.make_async_copy(
            blocks_ref.at[pl.ds(OWN, 4), :, lanes], far_f32.at[:, :, lanes], load_sem.at[n]))
    for n in range(own_chunks):
        lanes = pl.ds(n * span, span)
        loads.append(pltpu.make_async_copy(
            blocks_ref.at[pl.ds(0, OWN), :, lanes], own_f32.at[:, :, lanes], load_sem.at[far_chunks + n]))
    for load in loads:
        load.start()

    barrier = pltpu.get_barrier_semaphore()
    for d in range(1, n_mode):
        pl.semaphore_signal(barrier, inc=1, device_id=(me, lax.rem(my_mode + d, n_mode)), device_id_type=MESH)
    for d in range(1, n_dom):
        pl.semaphore_signal(barrier, inc=1, device_id=(lax.rem(me + d, n_dom), my_mode), device_id_type=MESH)

    for copy in small:
        copy.wait()
    f_nat = mass_ref[...] * source_ref[...]
    m_nat = mass_ref[...]
    w_nat = m_nat * f_nat
    pairs = clusters // 2
    pair_row = lax.broadcasted_iota(jnp.int32, (pairs, clusters), 0)
    cluster_col = lax.broadcasted_iota(jnp.int32, (pairs, clusters), 1)
    even = (cluster_col == 2 * pair_row).astype(F32)
    odd = (cluster_col == 2 * pair_row + 1).astype(F32)

    def across(nat):
        first = dot(nat, even, ((0,), (0,)), HIGHEST)
        second = dot(nat, odd, ((0,), (0,)), HIGHEST)
        return first[:width] + second[width:]

    def back(vec):
        first = dot(even, vec, ((1,), (1,)), HIGHEST)
        second = dot(odd, vec, ((1,), (1,)), HIGHEST)
        return jnp.concatenate([first, second], axis=1)

    m_t = across(m_nat)
    f_t = across(f_nat)
    w_t = m_t * f_t

    def spread(vectors, first, last):
        high = [v.astype(BF16).astype(F32) for v in vectors]
        packed = jnp.concatenate(high + [v - h for v, h in zip(vectors, high)], axis=1)
        lane = lax.rem(lax.broadcasted_iota(jnp.int32, packed.shape, 1), clusters)
        n = packed.shape[1]

        def place(g, carry):
            v_ref[pl.ds(pl.multiple_of(g * width, width), width), 0:n] = jnp.where(lane == g, packed, 0.0).astype(BF16)
            return carry
        lax.fori_loop(first, last, place, 0, unroll=8)

    spread([f_t, w_t], 0, clusters)

    lam_row = lam_ref[...]
    lam_tile = jnp.concatenate([column_of(lam_row), jnp.zeros((8 - md, 128), F32)], axis=0)
    lam_buf[0] = lam_tile
    def far_copies(out_buf, in_buf, send, recv):
        copies = []
        for h, offset in enumerate(OFFSETS):
            copies.append(pltpu.make_async_remote_copy(
                src_ref=out_buf.at[h], dst_ref=in_buf.at[h], send_sem=send.at[h], recv_sem=recv.at[h],
                device_id=(lax.rem(me + n_dom + offset, n_dom), my_mode), device_id_type=MESH))
        return copies

    def sum_copies(out_buf, in_buf, send, recv):
        copies = []
        for d in range(1, n_dom):
            copies.append(pltpu.make_async_remote_copy(
                src_ref=out_buf, dst_ref=in_buf.at[d - 1], send_sem=send.at[d - 1], recv_sem=recv.at[d - 1],
                device_id=(lax.rem(me + d, n_dom), my_mode), device_id_type=MESH))
        return copies

    def product(count, chunks, first_load, full, high, low, acc, n, first_pass):
        for c in range(chunks):
            lanes = pl.ds(c * span, span)
            if first_pass:
                loads[first_load + c].wait()
                hi, lo = halves(full[:, :, lanes].reshape(count * width, span))
                high[:, lanes] = hi
                low[:, lanes] = lo
            else:
                hi, lo = high[:, lanes], low[:, lanes]
            right = v_ref[lanes, 0:n]
            part = dot(hi, right) + dot(lo, right)
            if c:
                acc[:, 0:n] += part
            else:
                acc[:, 0:n] = part
        return acc[:, 0:n // 2] + acc[:, n // 2:n]

    cluster_row = lax.broadcasted_iota(jnp.int32, (clusters, clusters), 0)

    def collect(terms, vectors):
        total = terms[:width]
        high, low = halves(terms[width:])
        moved = None
        for s in range(1, OWN):
            hot = (cols_ref[s:s + 1, :] == cluster_row).astype(F32).astype(BF16)
            if vectors == 2:
                zero = jnp.zeros_like(hot)
                hot = jnp.concatenate([jnp.concatenate([hot, zero], 1), jnp.concatenate([zero, hot], 1)], 0)
            rows = slice((s - 1) * width, s * width)
            part = dot(high[rows], hot, ((1,), (1,))) + dot(low[rows], hot, ((1,), (1,)))
            moved = part if moved is None else moved + part
        return total + moved

    def widen(value):
        return jnp.concatenate([value, jnp.zeros((width, clusters - shared), F32)], axis=1)

    n1 = 4 * clusters
    terms = product(4, far_chunks, 0, far_f32, far_hi, far_lo, acc_far, n1, True)
    far1 = far_copies(far1_out, far1_in, far1_send, far1_recv)
    for h in range(4):
        rows = terms[h * width:(h + 1) * width]
        both = jnp.concatenate([rows[:, :shared], rows[:, clusters:clusters + shared]], axis=1)
        far1_out[h] = fold(both)
    wait_for = n_dom - 1 + n_mode - 1
    pl.semaphore_wait(barrier, wait_for)
    for copy in far1:
        copy.start()
    lam_copies = []
    for d in range(1, n_mode):
        copy = pltpu.make_async_remote_copy(
            src_ref=lam_buf.at[0], dst_ref=lam_buf.at[d], send_sem=lam_send.at[d], recv_sem=lam_recv.at[d],
            device_id=(me, lax.rem(my_mode + d, n_mode)), device_id_type=MESH)
        copy.start()
        lam_copies.append(copy)
    terms = product(OWN, own_chunks, far_chunks, own_f32, own_hi, own_lo, acc_own, n1, True)
    image = collect(terms, 2)
    for h in range(4):
        far1[h].wait_recv()
    arrived = unfold(far1_in[0] + far1_in[1] + far1_in[2] + far1_in[3])
    u_t = image[:, :clusters] + widen(arrived[:, :shared])
    q_t = image[:, clusters:] + widen(arrived[:, shared:])

    n2 = 2 * clusters
    spread([u_t], 0, shared)
    terms = product(4, far_chunks, 0, far_f32, far_hi, far_lo, acc_far, n2, False)
    far2 = far_copies(far2_out, far2_in, far2_send, far2_recv)
    for h in range(4):
        far2_out[h] = fold(fold(terms[h * width:(h + 1) * width, :shared]))
        far2[h].start()

    f_v, w_v, m_v, u_v, q_v = fold(f_t), fold(w_t), fold(m_t), fold(u_t), fold(q_t)

    def over(value):
        return jnp.sum(value, axis=0, keepdims=True)

    sum1_out[...] = jnp.concatenate(
        [over(f_v * f_v), over(f_v * u_v), over(f_v * w_v), jnp.zeros((5, 128), F32)], axis=0)
    sum1 = sum_copies(sum1_out, sum1_in, sum1_send, sum1_recv)
    for copy in sum1:
        copy.start()

    spread([u_t], shared, clusters)
    terms = product(OWN, own_chunks, far_chunks, own_f32, own_hi, own_lo, acc_own, n2, False)
    image = collect(terms, 1)

    for copy in lam_copies:
        copy.wait_recv()
    lam = jnp.zeros((md * n_mode, 128), F32)
    part_row = lax.broadcasted_iota(jnp.int32, (md * n_mode, 128), 0) // md
    for d in range(n_mode):
        own = lax.rem(my_mode + n_mode - d, n_mode)
        tiled = jnp.concatenate([lam_buf[d][:md]] * n_mode, axis=0)
        lam = jnp.where(part_row == own, tiled, lam)
    t = column_of(basis_ref[0:1, :])
    t2 = t * t

    for copy in sum1:
        copy.wait_recv()
    sums = sum1_out[...]
    for d in range(n_dom - 1):
        sums = sums + sum1_in[d]
    sums = jnp.broadcast_to(jnp.sum(sums, axis=1, keepdims=True), (8, 128))
    rr0 = t2 * sums[0:1]
    alpha = rr0 / (t2 * (sums[1:2] + lam * sums[2:3]))
    alpha_lam = alpha * lam

    residuals, squares, curves = [], [], []
    for k in range(modes):
        a, al = alpha[k:k + 1], alpha_lam[k:k + 1]
        r = f_v - a * u_v - al * w_v
        residuals.append((r, u_v - al * q_v + lam[k:k + 1] * (m_v * r)))
        squares.append(over(r * r))

    for h in range(4):
        far2[h].wait_recv()
    arrived = unfold(unfold(far2_in[0] + far2_in[1] + far2_in[2] + far2_in[3]))
    p_v = fold(image + widen(arrived))

    for k, (r, partial) in enumerate(residuals):
        curves.append(over(r * (partial - alpha[k:k + 1] * p_v)))
    sum2_out[...] = jnp.zeros((8, 128), F32)
    for row, parts in enumerate((squares, curves)):
        column = jnp.sum(jnp.concatenate(parts, axis=0), axis=1, keepdims=True)
        sum2_out[row:row + 1, 0:modes] = row_of(column)
    sum2 = sum_copies(sum2_out, sum2_in, sum2_send, sum2_recv)
    for copy in sum2:
        copy.start()

    u_nat = back(u_t)
    basis_own = jnp.concatenate(
        [basis_ref[pl.ds(my_mode * levels + level, 1), :] for level in range(levels)], axis=0)
    t_row = basis_ref[0:1, :]
    t2_row = t_row * t_row
    alpha_row, rr0_row, lam_row = row_of(alpha), row_of(rr0), row_of(lam)

    for copy in sum2:
        copy.wait_recv()
    sums = sum2_out[...]
    for d in range(n_dom - 1):
        sums = sums + sum2_in[d]
    rr1 = t2_row * sums[0:1, 0:modes]
    beta = rr1 / rr0_row
    alpha1 = rr1 / (t2_row * sums[1:2, 0:modes] - beta * (rr1 / alpha_row))
    coef_f = t_row * (alpha_row + alpha1 * (1.0 + beta))
    coef_u = -t_row * (alpha1 * alpha_row)
    coef_w = coef_u * lam_row
    c_f, c_u, c_w = (
        jnp.broadcast_to(jnp.sum(basis_own * c, axis=1, keepdims=True), (levels, 128))
        for c in (coef_f, coef_u, coef_w))
    for level in range(levels):
        one = slice(level, level + 1)
        out_ref[:, level, :] = c_f[one] * f_nat + c_u[one] * u_nat + c_w[one] * w_nat

    for copy in lam_copies + far1 + far2 + sum1 + sum2:
        copy.wait_send()


def solution(mesh):
    n_dom, n_mode = mesh.shape["dom"], mesh.shape["mode"]

    def body(source, mass, lambdas, trace_basis, blocks, columns):
        slots, width, vertices = blocks.shape
        clusters = columns.shape[0]
        shared = clusters // 2
        md = lambdas.shape[0]
        levels = LEVELS // n_mode
        lines = vertices // 128
        vmem = pl.BlockSpec(memory_space=pltpu.VMEM)
        hbm = pl.BlockSpec(memory_space=pltpu.HBM)
        dma = pltpu.SemaphoreType.DMA
        chunks = vertices // 1024 + shared * width // 1024
        result = pl.pallas_call(
            functools.partial(kernel, n_dom, n_mode),
            out_shape=pltpu.VMEM((lines, levels, 128), F32),
            in_specs=[hbm] * 6,
            out_specs=vmem,
            scratch_shapes=[
                pltpu.VMEM((lines, 128), F32),
                pltpu.VMEM((lines, 128), F32),
                pltpu.VMEM((1, md), F32),
                pltpu.VMEM(trace_basis.shape, F32),
                pltpu.VMEM((slots, clusters), jnp.int32),
                pltpu.VMEM((OWN, width, vertices), F32),
                pltpu.VMEM((slots - OWN, width, shared * width), F32),
                pltpu.VMEM((OWN * width, vertices), BF16),
                pltpu.VMEM((OWN * width, vertices), BF16),
                pltpu.VMEM(((slots - OWN) * width, shared * width), BF16),
                pltpu.VMEM(((slots - OWN) * width, shared * width), BF16),
                pltpu.VMEM((vertices, 4 * clusters), BF16),
                pltpu.VMEM((OWN * width, 4 * clusters), F32),
                pltpu.VMEM(((slots - OWN) * width, 4 * clusters), F32),
                pltpu.VMEM((n_mode, 8, 128), F32),
                pltpu.VMEM((4, width // 2, 2 * clusters), F32),
                pltpu.VMEM((4, width // 2, 2 * clusters), F32),
                pltpu.VMEM((4, width // 4, 4 * shared), F32),
                pltpu.VMEM((4, width // 4, 4 * shared), F32),
                pltpu.VMEM((8, 128), F32),
                pltpu.VMEM((n_dom - 1, 8, 128), F32),
                pltpu.VMEM((8, 128), F32),
                pltpu.VMEM((n_dom - 1, 8, 128), F32),
                dma((5,)),
                dma((chunks,)),
                dma((n_mode,)), dma((n_mode,)),
                dma((4,)), dma((4,)), dma((4,)), dma((4,)),
                dma((n_dom - 1,)), dma((n_dom - 1,)), dma((n_dom - 1,)), dma((n_dom - 1,)),
            ],
            compiler_params=pltpu.CompilerParams(
                collective_id=0, has_side_effects=True, vmem_limit_bytes=64 * 1024 * 1024 - 262144),
        )(
            source.reshape(lines, 128), mass.reshape(lines, 128), lambdas.reshape(1, md),
            trace_basis, blocks, columns.T,
        )
        return jnp.transpose(result, (1, 0, 2)).reshape(levels, vertices)

    in_specs = (P("dom"), P("dom"), P("mode"), P(), P(None, None, "dom"), P("dom", None))
    return jax.shard_map(body, mesh=mesh, in_specs=in_specs, out_specs=P("mode", "dom"), check_vma=False)
```
